32 devices in a mesh: beam: 2 (over y), tm: 4 (over z), chan: 2 (over x), pol: 2 (over core).
Axes of the slice: x: 2, y: 2, z: 4, core: 2. Of those that a mesh axis runs over, the one named last changes fastest.
Arguments:
- observed: float32 [2, 2, 64, 4096], P('pol', None, ('beam', 'tm'), 'chan'), parts along dimension 2, may hold values from -18 to 18
- window_taps: float32 [4, 4096], P(None, 'chan'), may hold values from -1.5 to 1.5
Outputs:
- estimate: float32 [2, 2, 64, 4096], P('pol', None, ('beam', 'tm'), 'chan'), parts along dimension 2
- residual: float32 [2, 2, 64, 4096], P('pol', None, ('beam', 'tm'), 'chan'), parts along dimension 2
The draws below stay inside these ranges and needn't reach their ends.
There are 2 independent parts, one for each index of `beam`. The reference program is written for one: setup_inputs(seed, part) draws one part's arguments, and reference() takes and returns one part's arrays. A program takes and returns all parts, laid end to end along the dimension named above; an argument that names none is the same for every part. Nothing has to cross between parts.
All inputs are finite; a program needn't handle non-finite values.
Results may differ from the reference program's by a relative error of at most 0.0003.
Values sent between devices are 32-bit elements; how exact they have to be, the bound alone decides.
A program may use at most 64 MiB of HBM per device.

```python
import jax
import jax.numpy as jnp

M = 4096
TAPS = 4
POLS = 2
ITERS = 2
FRAMES = 32


def draw_observed(key, part):
    key = jax.random.fold_in(key, 11)
    noise_key, band_key = jax.random.split(key)
    shape = (POLS, 2, FRAMES, M)
    noise = jax.random.truncated_normal(noise_key, -5.0, 5.0, shape, jnp.float32)
    rise = 3.0
    position = jnp.arange(FRAMES, dtype=jnp.float32) / max(FRAMES - 1, 1)
    envelope = jnp.exp(jnp.log(rise) * (position - 0.5))
    bandpass = jnp.exp(jax.random.uniform(band_key, (M,), jnp.float32, -0.69, 0.69))
    return noise * envelope[None, None, :, None] * bandpass[None, None, None, :]


def draw_window_taps(key, part):
    key = jax.random.fold_in(key, 23)
    lead_key, rest_key = jax.random.split(key)
    lead = jax.random.uniform(lead_key, (1, M), jnp.float32, 0.8, 1.4)
    others = 0.3 * jax.random.truncated_normal(rest_key, -5.0, 5.0, (TAPS - 1, M), jnp.float32)
    return jnp.concatenate([lead, others], axis=0)


def setup_inputs(seed: int = 0, part: int = 0) -> dict:
    arg_keys = jax.random.split(jax.random.key(seed), 3)
    part_splits = jax.random.split(jax.random.fold_in(arg_keys[2], part), 3)
    observed = draw_observed(jax.random.fold_in(jax.random.fold_in(arg_keys[2], part), 71), part)
    window_taps = draw_window_taps(jax.random.fold_in(arg_keys[2], 71), part)
    return {"observed": observed, "window_taps": window_taps}


def apply_window(signal, window_taps):
    frame_count = signal.shape[2]
    lead = window_taps.shape[0] - 1
    padded = jnp.pad(signal, ((0, 0), (0, 0), (lead, 0), (0, 0)))
    result = jnp.zeros_like(signal)
    for tap_index in range(lead + 1):
        first_row = lead - tap_index
        result = result + window_taps[tap_index][None, None, None, :] * padded[:, :, first_row:first_row + frame_count, :]
    return result


def window_transpose(signal, window_taps):
    frame_count = signal.shape[2]
    lead = window_taps.shape[0] - 1
    padded = jnp.pad(signal, ((0, 0), (0, 0), (0, lead), (0, 0)))
    result = jnp.zeros_like(signal)
    for tap_index in range(lead + 1):
        result = result + window_taps[tap_index][None, None, None, :] * padded[:, :, tap_index:tap_index + frame_count, :]
    return result


def spectrum_of(signal):
    values = signal[:, 0] + 1j * signal[:, 1]
    output = jnp.fft.fft(values, axis=-1, norm="ortho")
    return jnp.stack([jnp.real(output), jnp.imag(output)], axis=1).astype(signal.dtype)


def samples_of(signal):
    values = signal[:, 0] + 1j * signal[:, 1]
    output = jnp.fft.ifft(values, axis=-1, norm="ortho")
    return jnp.stack([jnp.real(output), jnp.imag(output)], axis=1).astype(signal.dtype)


def inner(left, right):
    return jnp.sum(left * right, axis=(1, 2, 3), keepdims=True)


def reference(observed, window_taps):
    estimate = jnp.zeros_like(observed)
    residual = observed
    gradient = window_transpose(samples_of(observed), window_taps)
    direction = gradient
    squares_now = inner(gradient, gradient)
    for iteration in range(ITERS):
        image = spectrum_of(apply_window(direction, window_taps))
        step_size = squares_now / inner(image, image)
        estimate = estimate + step_size * direction
        residual = residual - step_size * image
        if iteration + 1 < ITERS:
            gradient = window_transpose(samples_of(residual), window_taps)
            squares_next = inner(gradient, gradient)
            direction = gradient + (squares_next / squares_now) * direction
            squares_now = squares_next
    return estimate, residual
```

```python
import functools
import math

import jax
import jax.numpy as jnp
import ml_dtypes
import numpy as np
from jax import lax
from jax.experimental import pallas as pl
from jax.experimental.pallas import tpu as pltpu
from jax.sharding import PartitionSpec as P

LANES = 128
MESH = pl.DeviceIdType.MESH
F32 = jnp.float32
BF16 = jnp.bfloat16
STATS = 16


def dft_rows(values):
    count = len(values)
    if count == 1:
        return values
    even = dft_rows(values[::2])
    odd = dft_rows(values[1::2])
    low, high = [], []
    for k in range(count // 2):
        er, ei = even[k]
        xr, xi = odd[k]
        if k == 0:
            tr, ti = xr, xi
        elif 4 * k == count:
            tr, ti = -xi, xr
        elif 8 * k == count:
            h = math.sqrt(0.5)
            tr, ti = h * (xr - xi), h * (xr + xi)
        elif 8 * k == 3 * count:
            h = math.sqrt(0.5)
            tr, ti = -h * (xr + xi), h * (xr - xi)
        else:
            cs = math.cos(2 * math.pi * k / count)
            sn = math.sin(2 * math.pi * k / count)
            tr, ti = cs * xr - sn * xi, sn * xr + cs * xi
        low.append((er + tr, ei + ti))
        high.append((er - tr, ei - ti))
    return low + high


def halves(value):
    high = value.astype(BF16)
    return high, (value - high.astype(F32)).astype(BF16)


def dot(left, right):
    return jnp.dot(left, right, preferred_element_type=F32)


def kernel(
    n,
    shards_t,
    obs_ref,
    taps_ref,
    whi_ref,
    wlo_ref,
    tw_ref,
    place_ref,
    perm_ref,
    est_ref,
    res_ref,
    xb,
    hb,
    tb,
    tp,
    zr,
    zi,
    yo,
    yh,
    dd,
    fr,
    es,
    ar,
    sx,
    rx,
    st,
    rt,
    sz,
    rz,
    sa,
    ra,
):
    frames = obs_ref.shape[2]
    taps = taps_ref.shape[0]
    lead = taps - 1
    halo = 2 * lead
    rad = zr.shape[0] // frames
    per = rad // n
    rows = 2 * per
    xs, hs, ts = frames * rows, 2 * halo * rows, taps * per
    c = lax.axis_index("chan")
    t = lax.axis_index("tm")
    has_prev = t > 0
    has_next = t < shards_t - 1

    barrier = pltpu.get_barrier_semaphore()
    for d in range(1, n):
        pl.semaphore_signal(
            barrier, inc=1, device_id={"chan": lax.rem(c + d, n)}, device_id_type=MESH
        )
    for d in range(1, shards_t):
        pl.semaphore_signal(
            barrier, inc=1, device_id={"tm": lax.rem(t + d, shards_t)}, device_id_type=MESH
        )

    for part in range(2):
        for k in range(per):
            xb[pl.ds(c * xs + part * per + k, frames, stride=rows), :] = obs_ref[
                0, part, :, k * LANES : (k + 1) * LANES
            ]
    for k in range(per):
        tb[pl.ds(c * ts + k, taps, stride=per), :] = taps_ref[:, k * LANES : (k + 1) * LANES]

    @pl.when(jnp.logical_not(has_prev))
    def _():
        for j in range(n):
            hb[j * hs : j * hs + halo * rows, :] = jnp.zeros((halo * rows, LANES), F32)

    @pl.when(jnp.logical_not(has_next))
    def _():
        for j in range(n):
            hb[j * hs + halo * rows : (j + 1) * hs, :] = jnp.zeros((halo * rows, LANES), F32)

    pl.semaphore_wait(barrier, n - 1 + shards_t - 1)

    def along_x(d):
        block = xb.at[pl.ds(pl.multiple_of(c * xs, 8), xs), :]
        return pltpu.make_async_remote_copy(
            src_ref=block,
            dst_ref=block,
            send_sem=sx.at[d],
            recv_sem=rx.at[d],
            device_id={"chan": lax.rem(c + d, n)},
            device_id_type=MESH,
        )

    def taps_x(d):
        block = tb.at[pl.ds(pl.multiple_of(c * ts, 8), ts), :]
        return pltpu.make_async_remote_copy(
            src_ref=block,
            dst_ref=block,
            send_sem=st.at[d],
            recv_sem=rt.at[d],
            device_id={"chan": lax.rem(c + d, n)},
            device_id_type=MESH,
        )

    def to_next(d):
        j = lax.rem(c - d + n, n)
        size = halo * rows
        return pltpu.make_async_remote_copy(
            src_ref=xb.at[pl.ds(pl.multiple_of(j * xs + (frames - halo) * rows, 8), size), :],
            dst_ref=hb.at[pl.ds(pl.multiple_of(j * hs, 8), size), :],
            send_sem=sz.at[0, d],
            recv_sem=rz.at[0, d],
            device_id={"tm": lax.rem(t + 1, shards_t)},
            device_id_type=MESH,
        )

    def to_prev(d):
        j = lax.rem(c - d + n, n)
        size = halo * rows
        return pltpu.make_async_remote_copy(
            src_ref=xb.at[pl.ds(pl.multiple_of(j * xs, 8), size), :],
            dst_ref=hb.at[pl.ds(pl.multiple_of(j * hs + size, 8), size), :],
            send_sem=sz.at[1, d],
            recv_sem=rz.at[1, d],
            device_id={"tm": lax.rem(t + shards_t - 1, shards_t)},
            device_id_type=MESH,
        )

    def start_halo(d):
        @pl.when(has_next)
        def _():
            to_next(d).start()

        @pl.when(has_prev)
        def _():
            to_prev(d).start()

    for d in range(1, n):
        along_x(d).start()
    start_halo(0)
    for d in range(1, n):
        taps_x(d).start()
    for d in range(1, n):
        along_x(d).wait_recv()
        start_halo(d)

    def lanes_dft(real, imag):
        hi, lo = halves(jnp.concatenate([real, imag], axis=1))
        whi = whi_ref[...]
        return dot(hi, whi) + dot(lo, whi) + dot(hi, wlo_ref[...])

    def samples(src, stride, first):
        values = []
        for k in range(rad):
            base = (k // per) * stride + first * rows + k % per
            values.append(
                tuple(
                    src[pl.ds(base + part * per, frames, stride=rows), :] for part in range(2)
                )
            )
        for m, (re, im) in enumerate(dft_rows(values)):
            cs, sn = tw_ref[0, m : m + 1, :], tw_ref[1, m : m + 1, :]
            zr[pl.ds(m, frames, stride=rad), :] = re * cs - im * sn
            zi[pl.ds(m, frames, stride=rad), :] = re * sn + im * cs
        return lanes_dft(zr[...], zi[...])

    out = samples(xb, xs, 0)
    yo[0] = out[:, :LANES]
    yo[1] = out[:, LANES:]

    for d in range(1, n):
        taps_x(d).wait_recv()
    turned = tb[...].T
    first = turned.astype(BF16)
    rest = turned - first.astype(F32)
    second = rest.astype(BF16)
    third = (rest - second.astype(F32)).astype(BF16)
    placed = jnp.zeros((rad, taps * LANES), F32)
    for s in range(LANES // rad):
        rng = slice(s * rad, (s + 1) * rad)
        for piece in (third, second, first):
            placed = placed + dot(piece[rng, :], place_ref[s])
    for p in range(taps):
        tp[p * rad : (p + 1) * rad, :] = placed[:, p * LANES : (p + 1) * LANES]

    @pl.when(has_prev)
    def _():
        for d in range(n):
            to_next(d).wait_recv()

    @pl.when(has_next)
    def _():
        for d in range(n):
            to_prev(d).wait_recv()

    shift = 2 * halo - frames

    def halo_step(i, carry):
        begin = i * shift
        out = samples(hb, hs, begin)
        at = pl.ds(pl.multiple_of(begin * rad, 8), frames * rad)
        yh[0, at, :] = out[:, :LANES]
        yh[1, at, :] = out[:, LANES:]
        return carry

    lax.fori_loop(0, 2, halo_step, 0)

    keep_prev = jnp.where(has_prev, 1.0, 0.0).astype(F32)
    keep_next = jnp.where(has_next, 1.0, 0.0).astype(F32)
    chunks = rad // 8

    def window_step(i, carry):
        s0, s1 = carry
        part = i // chunks
        ch = i % chunks

        def at(f):
            return pl.ds(pl.multiple_of(f * rad + ch * 8, 8), 8)

        def signal(f):
            if f < 0:
                return yh[part, at(f + halo), :]
            if f < frames:
                return yo[part, at(f), :]
            return yh[part, at(f - frames + halo), :]

        w = [tp[at(p), :] for p in range(taps)]

        def ahead(x, f):
            return sum(w[p] * x[f + p] for p in range(1, taps)) + w[0] * x[f]

        def behind(x, f):
            return sum(w[p] * x[f - p] for p in range(1, taps)) + w[0] * x[f]

        y = {f: signal(f) for f in range(-halo, frames + halo)}
        g = {f: ahead(y, f) for f in range(-halo, frames + lead)}
        g = {f: (v * keep_prev if f < 0 else v) for f, v in g.items()}
        v = {f: behind(g, f) for f in range(-lead, frames + lead)}
        v = {f: (x * keep_next if f >= frames else x) for f, x in v.items()}
        z = {f: ahead(v, f) for f in range(-lead, frames)}
        z = {f: (x * keep_prev if f < 0 else x) for f, x in z.items()}
        for f in range(frames):
            dd[0, part, at(f), :] = g[f]
            dd[1, part, at(f), :] = z[f]
            dd[2, part, at(f), :] = v[f]
            dd[3, part, at(f), :] = behind(z, f)
            s0 = s0 + g[f] * g[f]
            s1 = s1 + v[f] * v[f]
        return s0, s1

    zero = jnp.zeros((8, LANES), F32)
    s0, s1 = lax.fori_loop(0, 2 * chunks, window_step, (zero, zero))
    s0 = jnp.sum(s0, keepdims=True)
    s1 = jnp.sum(s1, keepdims=True)
    center = jnp.where(s1 > 0, s0 / jnp.where(s1 > 0, s1, 1.0), 0.0)

    def moment_step(i, carry):
        pp, pz, zz, qq, qu, uu = carry
        part = i // chunks
        ch = i % chunks
        for f in range(frames):
            at = pl.ds(pl.multiple_of(f * rad + ch * 8, 8), 8)
            z, u = dd[1, part, at, :], dd[3, part, at, :]
            p = dd[0, part, at, :] - center * z
            q = dd[2, part, at, :] - center * u
            pp, pz, zz = pp + p * p, pz + p * z, zz + z * z
            qq, qu, uu = qq + q * q, qu + q * u, uu + u * u
        return pp, pz, zz, qq, qu, uu

    moments = lax.fori_loop(0, 2 * chunks, moment_step, (zero,) * 6)
    moments = [jnp.sum(x, keepdims=True) for x in moments]
    line = jnp.concatenate(
        [jnp.broadcast_to(x, (1, LANES)) for x in [s0, s1, center] + moments]
        + [jnp.zeros((STATS - 9, LANES), F32)],
        axis=0,
    )
    mine = pl.ds(pl.multiple_of(t * STATS, 8), STATS)
    ar[mine, :] = line

    def sums_to(d):
        return pltpu.make_async_remote_copy(
            src_ref=ar.at[mine, :],
            dst_ref=ar.at[mine, :],
            send_sem=sa.at[d],
            recv_sem=ra.at[d],
            device_id={"tm": lax.rem(t + d, shards_t)},
            device_id_type=MESH,
        )

    for d in range(1, shards_t):
        sums_to(d).start()

    def spectrum_step(a, carry):
        out = lanes_dft(dd[2 + a, 0], -dd[2 + a, 1])
        for f in range(frames):
            at = slice(f * rad, (f + 1) * rad)
            re, im = out[at, :LANES], out[at, LANES:]
            zr[at, :] = re * tw_ref[0] - im * tw_ref[1]
            zi[at, :] = re * tw_ref[1] + im * tw_ref[0]
        values = [
            (zr[pl.ds(m, frames, stride=rad), :], zi[pl.ds(m, frames, stride=rad), :])
            for m in range(rad)
        ]
        for k, (re, im) in enumerate(dft_rows(values)):
            fr[a, 0, k * frames : (k + 1) * frames, :] = re
            fr[a, 1, k * frames : (k + 1) * frames, :] = im
        hi, lo = halves(jnp.concatenate([dd[a, 0], dd[a, 1]], axis=1))
        perm = perm_ref[c]
        moved = dot(hi, perm) + dot(lo, perm)
        quad = LANES // rad
        for h in range(frames // quad):
            flat = moved[h * LANES : (h + 1) * LANES, :].T
            for part in range(2):
                for f in range(quad):
                    joined = jnp.concatenate(
                        [
                            flat[
                                (part * quad + s) * per : (part * quad + s + 1) * per,
                                f * rad : (f + 1) * rad,
                            ]
                            for s in range(quad)
                        ],
                        axis=1,
                    )
                    row = (part * frames + h * quad + f) * per
                    es[a, row : row + per, :] = joined
        return carry

    lax.fori_loop(0, 2, spectrum_step, 0)

    for d in range(1, shards_t):
        sums_to(d).wait_recv()

    def total(i):
        return sum(ar[s * STATS + i : s * STATS + i + 1, :] for s in range(shards_t))

    gamma0 = total(0)
    step0 = gamma0 / total(1)
    gamma1 = jnp.zeros((1, LANES), F32)
    grown = jnp.zeros((1, LANES), F32)
    for s in range(shards_t):
        line = ar[s * STATS : (s + 1) * STATS, :]
        away = step0 - line[2:3]
        gamma1 = gamma1 + (line[3:4] - away * (2.0 * line[4:5] - away * line[5:6]))
        grown = grown + (line[6:7] - away * (2.0 * line[7:8] - away * line[8:9]))
    ratio = gamma1 / gamma0
    step1 = gamma1 / (grown - ratio * gamma1 / step0)
    near = step0 + step1 * (1.0 + ratio)
    far = step0 * step1

    for part in range(2):
        for k in range(per):
            at = pl.ds(pl.multiple_of((c * per + k) * frames, 8), frames)
            change = near * fr[0, part, at, :] - far * fr[1, part, at, :]
            here = obs_ref[0, part, :, k * LANES : (k + 1) * LANES]
            res_ref[0, part, :, k * LANES : (k + 1) * LANES] = (
                here - change if part == 0 else here + change
            )
            at = pl.ds(part * frames * per + k, frames, stride=per)
            est_ref[0, part, :, k * LANES : (k + 1) * LANES] = near * es.at[0][at, :] - far * es.at[
                1
            ][at, :]

    for d in range(1, n):
        along_x(d).wait_send()
        taps_x(d).wait_send()
    for d in range(1, shards_t):
        sums_to(d).wait_send()

    @pl.when(has_next)
    def _():
        for d in range(n):
            to_next(d).wait_send()

    @pl.when(has_prev)
    def _():
        for d in range(n):
            to_prev(d).wait_send()


def tables(n, rad, taps):
    whole = rad * LANES
    index = np.arange(LANES)
    angle = 2.0 * np.pi * (np.outer(index, index) % LANES) / LANES
    cs, sn = np.cos(angle) / math.sqrt(whole), np.sin(angle) / math.sqrt(whole)
    weights = np.block([[cs, sn], [-sn, cs]]).astype(np.float32)
    high = weights.astype(ml_dtypes.bfloat16)
    low = (weights - high.astype(np.float32)).astype(ml_dtypes.bfloat16)
    angle = 2.0 * np.pi * np.outer(np.arange(rad), index) / whole
    twist = np.stack([np.cos(angle), np.sin(angle)]).astype(np.float32)
    per = rad // n
    quad = LANES // rad
    place = np.zeros((quad, taps * rad, taps * LANES), ml_dtypes.bfloat16)
    perm = np.zeros((n, 2 * LANES, 2 * quad * per), ml_dtypes.bfloat16)
    for j in range(n):
        for k in range(per):
            for s in range(quad):
                lane = quad * (j * per + k) + s
                for p in range(taps):
                    place[s, (j * taps + p) * per + k, p * LANES + lane] = 1
                for part in range(2):
                    perm[j, part * LANES + lane, (part * quad + s) * per + k] = 1
    return high, low, twist, place, perm


def shards(n, shards_t, observed, window_taps):
    frames = observed.shape[2]
    taps = window_taps.shape[0]
    rad = observed.shape[3] * n // LANES
    halo = 2 * (taps - 1)
    assert frames == 8 and halo <= frames <= 2 * halo and taps * rad == LANES
    constants = tables(n, rad, taps)
    vmem = pl.BlockSpec(memory_space=pltpu.VMEM)
    dma = pltpu.SemaphoreType.DMA
    return pl.pallas_call(
        functools.partial(kernel, n, shards_t),
        out_shape=(jax.ShapeDtypeStruct(observed.shape, F32),) * 2,
        in_specs=[vmem] * 7,
        out_specs=(vmem, vmem),
        scratch_shapes=[
            pltpu.VMEM((frames * 2 * rad, LANES), F32),
            pltpu.VMEM((2 * halo * 2 * rad, LANES), F32),
            pltpu.VMEM((taps * rad, LANES), F32),
            pltpu.VMEM((taps * rad, LANES), F32),
            pltpu.VMEM((frames * rad, LANES), F32),
            pltpu.VMEM((frames * rad, LANES), F32),
            pltpu.VMEM((2, frames * rad, LANES), F32),
            pltpu.VMEM((2, 2 * halo * rad, LANES), F32),
            pltpu.VMEM((4, 2, frames * rad, LANES), F32),
            pltpu.VMEM((2, 2, frames * rad, LANES), F32),
            pltpu.VMEM((2, 2 * frames * rad // n, LANES), F32),
            pltpu.VMEM((shards_t * STATS, LANES), F32),
            dma((n,)),
            dma((n,)),
            dma((n,)),
            dma((n,)),
            dma((2, n)),
            dma((2, n)),
            dma((shards_t,)),
            dma((shards_t,)),
        ],
        compiler_params=pltpu.CompilerParams(
            collective_id=0, has_side_effects=True, vmem_limit_bytes=32 * 1024 * 1024
        ),
        cost_estimate=pl.CostEstimate(flops=10**9, bytes_accessed=10**6, transcendentals=0),
    )(observed, window_taps, *(jnp.asarray(x) for x in constants))


def solution(mesh):
    n, shards_t = mesh.shape["chan"], mesh.shape["tm"]
    block = P("pol", None, ("beam", "tm"), "chan")
    return jax.shard_map(
        functools.partial(shards, n, shards_t),
        mesh=mesh,
        in_specs=(block, P(None, "chan")),
        out_specs=(block, block),
        check_vma=False,
    )
```

```python
import functools
import math

import jax
import jax.numpy as jnp
import ml_dtypes
import numpy as np
from jax import lax
from jax.experimental import pallas as pl
from jax.experimental.pallas import tpu as pltpu
from jax.sharding import PartitionSpec as P

LANES = 128
MESH = pl.DeviceIdType.MESH
F32 = jnp.float32
BF16 = jnp.bfloat16
STATS = 16


def dft_rows(values):
    count = len(values)
    if count == 1:
        return values
    even = dft_rows(values[::2])
    odd = dft_rows(values[1::2])
    low, high = [], []
    for k in range(count // 2):
        er, ei = even[k]
        xr, xi = odd[k]
        if k == 0:
            tr, ti = xr, xi
        elif 4 * k == count:
            tr, ti = -xi, xr
        elif 8 * k == count:
            h = math.sqrt(0.5)
            tr, ti = h * (xr - xi), h * (xr + xi)
        elif 8 * k == 3 * count:
            h = math.sqrt(0.5)
            tr, ti = -h * (xr + xi), h * (xr - xi)
        else:
            cs = math.cos(2 * math.pi * k / count)
            sn = math.sin(2 * math.pi * k / count)
            tr, ti = cs * xr - sn * xi, sn * xr + cs * xi
        low.append((er + tr, ei + ti))
        high.append((er - tr, ei - ti))
    return low + high


def halves(value):
    high = value.astype(BF16)
    return high, (value - high.astype(F32)).astype(BF16)


def dot(left, right):
    return jnp.dot(left, right, preferred_element_type=F32)


def kernel(
    n,
    shards_t,
    obs_hbm,
    taps_hbm,
    whi_hbm,
    wlo_hbm,
    tw_hbm,
    place_hbm,
    perm_hbm,
    est_ref,
    res_ref,
    obs_ref,
    taps_ref,
    whi_ref,
    wlo_ref,
    tw_ref,
    place_ref,
    perm_ref,
    lo,
    xb,
    hb,
    tb,
    tp,
    zr,
    zi,
    yo,
    yh,
    dd,
    fr,
    es,
    ar,
    sx,
    rx,
    st,
    rt,
    sz,
    rz,
    sa,
    ra,
):
    loads = [
        pltpu.make_async_copy(src, dst, lo.at[i])
        for i, (src, dst) in enumerate(
            [
                (obs_hbm, obs_ref),
                (taps_hbm, taps_ref),
                (tw_hbm, tw_ref),
                (whi_hbm, whi_ref),
                (wlo_hbm, wlo_ref),
                (place_hbm, place_ref),
                (perm_hbm, perm_ref),
            ]
        )
    ]
    for load in loads:
        load.start()
    frames = obs_ref.shape[2]
    taps = taps_ref.shape[0]
    lead = taps - 1
    halo = 2 * lead
    rad = zr.shape[0] // frames
    per = rad // n
    rows = 2 * per
    step = frames - halo
    pieces = [*range(step, frames - step, step), 0, frames - step]
    xs, hs, ts = frames * rows, 2 * halo * rows, taps * per
    c = lax.axis_index("chan")
    t = lax.axis_index("tm")
    has_prev = t > 0
    has_next = t < shards_t - 1

    barrier = pltpu.get_barrier_semaphore()
    for d in range(1, n):
        pl.semaphore_signal(
            barrier, inc=1, device_id={"chan": lax.rem(c + d, n)}, device_id_type=MESH
        )
    for d in range(1, shards_t):
        pl.semaphore_signal(
            barrier, inc=1, device_id={"tm": lax.rem(t + d, shards_t)}, device_id_type=MESH
        )

    loads[0].wait()
    for part in range(2):
        for k in range(per):
            xb[pl.ds(c * xs + part * per + k, frames, stride=rows), :] = obs_ref[
                0, part, :, k * LANES : (k + 1) * LANES
            ]
    loads[1].wait()
    for k in range(per):
        tb[pl.ds(c * ts + k, taps, stride=per), :] = taps_ref[:, k * LANES : (k + 1) * LANES]

    @pl.when(jnp.logical_not(has_prev))
    def _():
        for j in range(n):
            hb[j * hs : j * hs + halo * rows, :] = jnp.zeros((halo * rows, LANES), F32)

    @pl.when(jnp.logical_not(has_next))
    def _():
        for j in range(n):
            hb[j * hs + halo * rows : (j + 1) * hs, :] = jnp.zeros((halo * rows, LANES), F32)

    pl.semaphore_wait(barrier, n - 1 + shards_t - 1)

    def along_x(d, q):
        block = xb.at[pl.ds(pl.multiple_of(c * xs + pieces[q] * rows, 8), step * rows), :]
        return pltpu.make_async_remote_copy(
            src_ref=block,
            dst_ref=block,
            send_sem=sx.at[d, q],
            recv_sem=rx.at[d, q],
            device_id={"chan": lax.rem(c + d, n)},
            device_id_type=MESH,
        )

    def taps_x(d):
        block = tb.at[pl.ds(pl.multiple_of(c * ts, 8), ts), :]
        return pltpu.make_async_remote_copy(
            src_ref=block,
            dst_ref=block,
            send_sem=st.at[d],
            recv_sem=rt.at[d],
            device_id={"chan": lax.rem(c + d, n)},
            device_id_type=MESH,
        )

    def along_z(way, d, q, first, last):
        j = lax.rem(c - d + n, n)
        slot = first - (frames - halo) if way == 0 else halo + first
        size = (last - first) * rows
        return pltpu.make_async_remote_copy(
            src_ref=xb.at[pl.ds(pl.multiple_of(j * xs + first * rows, 8), size), :],
            dst_ref=hb.at[pl.ds(pl.multiple_of(j * hs + slot * rows, 8), size), :],
            send_sem=sz.at[way, d, q],
            recv_sem=rz.at[way, d, q],
            device_id={"tm": lax.rem(t + (1 if way == 0 else shards_t - 1), shards_t)},
            device_id_type=MESH,
        )

    spans = ((frames - halo, frames), (0, halo))
    forward = [[], []]
    for way in range(2):
        forward[way].append((0, 0) + spans[way])
        for d in range(1, n):
            for q, f in enumerate(pieces):
                if spans[way][0] <= f < spans[way][1]:
                    forward[way].append((d, q, f, f + step))
    sends_to = (has_next, has_prev)
    gets_from = (has_prev, has_next)

    def start_halo(d, q):
        for way in range(2):
            for move in forward[way]:
                if move[:2] == (d, q):

                    @pl.when(sends_to[way])
                    def _(way=way, move=move):
                        along_z(way, *move).start()

    for q in range(len(pieces)):
        for d in range(1, n):
            along_x(d, q).start()
    start_halo(0, 0)
    for load in loads[2:]:
        load.wait()
    for q in range(len(pieces)):
        for d in range(1, n):
            along_x(d, q).wait_recv()
            start_halo(d, q)
    for d in range(1, n):
        taps_x(d).start()

    def lanes_dft(real, imag):
        hi, lo = halves(jnp.concatenate([real, imag], axis=1))
        whi = whi_ref[...]
        return dot(hi, whi) + dot(lo, whi) + dot(hi, wlo_ref[...])

    def samples(src, stride, first):
        values = []
        for k in range(rad):
            base = (k // per) * stride + first * rows + k % per
            values.append(
                tuple(
                    src[pl.ds(base + part * per, frames, stride=rows), :] for part in range(2)
                )
            )
        for m, (re, im) in enumerate(dft_rows(values)):
            cs, sn = tw_ref[0, m : m + 1, :], tw_ref[1, m : m + 1, :]
            zr[pl.ds(m, frames, stride=rad), :] = re * cs - im * sn
            zi[pl.ds(m, frames, stride=rad), :] = re * sn + im * cs
        return lanes_dft(zr[...], zi[...])

    out = samples(xb, xs, 0)
    yo[0] = out[:, :LANES]
    yo[1] = out[:, LANES:]

    for d in range(1, n):
        taps_x(d).wait_recv()
    turned = tb[...].T
    first = turned.astype(BF16)
    rest = turned - first.astype(F32)
    second = rest.astype(BF16)
    third = (rest - second.astype(F32)).astype(BF16)
    placed = jnp.zeros((rad, taps * LANES), F32)
    for s in range(LANES // rad):
        rng = slice(s * rad, (s + 1) * rad)
        for piece in (third, second, first):
            placed = placed + dot(piece[rng, :], place_ref[s])
    for p in range(taps):
        tp[p * rad : (p + 1) * rad, :] = placed[:, p * LANES : (p + 1) * LANES]

    for way in range(2):

        @pl.when(gets_from[way])
        def _(way=way):
            for move in forward[way]:
                along_z(way, *move).wait_recv()

    shift = 2 * halo - frames

    def halo_step(i, carry):
        begin = i * shift
        out = samples(hb, hs, begin)
        at = pl.ds(pl.multiple_of(begin * rad, 8), frames * rad)
        yh[0, at, :] = out[:, :LANES]
        yh[1, at, :] = out[:, LANES:]
        return carry

    lax.fori_loop(0, 2, halo_step, 0)

    keep_prev = jnp.where(has_prev, 1.0, 0.0).astype(F32)
    keep_next = jnp.where(has_next, 1.0, 0.0).astype(F32)
    chunks = rad // 8

    def window_step(i, carry):
        s0, s1 = carry
        part = i // chunks
        ch = i % chunks

        def at(f):
            return pl.ds(pl.multiple_of(f * rad + ch * 8, 8), 8)

        def signal(f):
            if f < 0:
                return yh[part, at(f + halo), :]
            if f < frames:
                return yo[part, at(f), :]
            return yh[part, at(f - frames + halo), :]

        w = [tp[at(p), :] for p in range(taps)]

        def ahead(x, f):
            return sum(w[p] * x[f + p] for p in range(1, taps)) + w[0] * x[f]

        def behind(x, f):
            return sum(w[p] * x[f - p] for p in range(1, taps)) + w[0] * x[f]

        y = {f: signal(f) for f in range(-halo, frames + halo)}
        g = {f: ahead(y, f) for f in range(-halo, frames + lead)}
        g = {f: (v * keep_prev if f < 0 else v) for f, v in g.items()}
        v = {f: behind(g, f) for f in range(-lead, frames + lead)}
        v = {f: (x * keep_next if f >= frames else x) for f, x in v.items()}
        z = {f: ahead(v, f) for f in range(-lead, frames)}
        z = {f: (x * keep_prev if f < 0 else x) for f, x in z.items()}
        for f in range(frames):
            dd[0, part, at(f), :] = g[f]
            dd[1, part, at(f), :] = z[f]
            dd[2, part, at(f), :] = v[f]
            dd[3, part, at(f), :] = behind(z, f)
            s0 = s0 + g[f] * g[f]
            s1 = s1 + v[f] * v[f]
        return s0, s1

    zero = jnp.zeros((8, LANES), F32)
    s0, s1 = lax.fori_loop(0, 2 * chunks, window_step, (zero, zero))
    s0 = jnp.sum(s0, keepdims=True)
    s1 = jnp.sum(s1, keepdims=True)
    center = jnp.where(s1 > 0, s0 / jnp.where(s1 > 0, s1, 1.0), 0.0)

    def moment_step(i, carry):
        pp, pz, zz, qq, qu, uu = carry
        part = i // chunks
        ch = i % chunks
        for f in range(frames):
            at = pl.ds(pl.multiple_of(f * rad + ch * 8, 8), 8)
            z, u = dd[1, part, at, :], dd[3, part, at, :]
            p = dd[0, part, at, :] - center * z
            q = dd[2, part, at, :] - center * u
            pp, pz, zz = pp + p * p, pz + p * z, zz + z * z
            qq, qu, uu = qq + q * q, qu + q * u, uu + u * u
        return pp, pz, zz, qq, qu, uu

    moments = lax.fori_loop(0, 2 * chunks, moment_step, (zero,) * 6)
    moments = [jnp.sum(x, keepdims=True) for x in moments]
    line = jnp.concatenate(
        [jnp.broadcast_to(x, (1, LANES)) for x in [s0, s1, center] + moments]
        + [jnp.zeros((STATS - 9, LANES), F32)],
        axis=0,
    )
    mine = pl.ds(pl.multiple_of(t * STATS, 8), STATS)
    ar[mine, :] = line

    def sums_to(d):
        return pltpu.make_async_remote_copy(
            src_ref=ar.at[mine, :],
            dst_ref=ar.at[mine, :],
            send_sem=sa.at[d],
            recv_sem=ra.at[d],
            device_id={"tm": lax.rem(t + d, shards_t)},
            device_id_type=MESH,
        )

    for d in range(1, shards_t):
        sums_to(d).start()

    def spectrum_step(a, carry):
        out = lanes_dft(dd[2 + a, 0], -dd[2 + a, 1])
        for f in range(frames):
            at = slice(f * rad, (f + 1) * rad)
            re, im = out[at, :LANES], out[at, LANES:]
            zr[at, :] = re * tw_ref[0] - im * tw_ref[1]
            zi[at, :] = re * tw_ref[1] + im * tw_ref[0]
        values = [
            (zr[pl.ds(m, frames, stride=rad), :], zi[pl.ds(m, frames, stride=rad), :])
            for m in range(rad)
        ]
        for k, (re, im) in enumerate(dft_rows(values)):
            fr[a, 0, k * frames : (k + 1) * frames, :] = re
            fr[a, 1, k * frames : (k + 1) * frames, :] = im
        hi, lo = halves(jnp.concatenate([dd[a, 0], dd[a, 1]], axis=1))
        perm = perm_ref[c]
        moved = dot(hi, perm) + dot(lo, perm)
        quad = LANES // rad
        for h in range(frames // quad):
            flat = moved[h * LANES : (h + 1) * LANES, :].T
            for part in range(2):
                for f in range(quad):
                    joined = jnp.concatenate(
                        [
                            flat[
                                (part * quad + s) * per : (part * quad + s + 1) * per,
                                f * rad : (f + 1) * rad,
                            ]
                            for s in range(quad)
                        ],
                        axis=1,
                    )
                    row = (part * frames + h * quad + f) * per
                    es[a, row : row + per, :] = joined
        return carry

    lax.fori_loop(0, 2, spectrum_step, 0)

    for d in range(1, shards_t):
        sums_to(d).wait_recv()

    def total(i):
        return sum(ar[s * STATS + i : s * STATS + i + 1, :] for s in range(shards_t))

    gamma0 = total(0)
    step0 = gamma0 / total(1)
    gamma1 = jnp.zeros((1, LANES), F32)
    grown = jnp.zeros((1, LANES), F32)
    for s in range(shards_t):
        line = ar[s * STATS : (s + 1) * STATS, :]
        away = step0 - line[2:3]
        gamma1 = gamma1 + (line[3:4] - away * (2.0 * line[4:5] - away * line[5:6]))
        grown = grown + (line[6:7] - away * (2.0 * line[7:8] - away * line[8:9]))
    ratio = gamma1 / gamma0
    step1 = gamma1 / (grown - ratio * gamma1 / step0)
    near = step0 + step1 * (1.0 + ratio)
    far = step0 * step1

    for part in range(2):
        for k in range(per):
            at = pl.ds(pl.multiple_of((c * per + k) * frames, 8), frames)
            change = near * fr[0, part, at, :] - far * fr[1, part, at, :]
            here = obs_ref[0, part, :, k * LANES : (k + 1) * LANES]
            res_ref[0, part, :, k * LANES : (k + 1) * LANES] = (
                here - change if part == 0 else here + change
            )
            at = pl.ds(part * frames * per + k, frames, stride=per)
            est_ref[0, part, :, k * LANES : (k + 1) * LANES] = near * es.at[0][at, :] - far * es.at[
                1
            ][at, :]

    for d in range(1, n):
        for q in range(len(pieces)):
            along_x(d, q).wait_send()
        taps_x(d).wait_send()
    for d in range(1, shards_t):
        sums_to(d).wait_send()
    for way in range(2):

        @pl.when(sends_to[way])
        def _(way=way):
            for move in forward[way]:
                along_z(way, *move).wait_send()


def place_results(est_in, res_in, est_out, res_out, est_buf, res_buf, sems):
    moves = []
    for src, buf, dst in ((est_in, est_buf, est_out), (res_in, res_buf, res_out)):
        for part in range(2):
            i = len(moves)
            moves.append(
                (
                    pltpu.make_async_copy(src.at[0, part], buf.at[part], sems.at[0, i]),
                    pltpu.make_async_copy(buf.at[part], dst.at[0, part], sems.at[1, i]),
                )
            )
    for load, _ in moves:
        load.start()
    for load, store in moves:
        load.wait()
        store.start()
    for _, store in moves:
        store.wait()


def tables(n, rad, taps):
    whole = rad * LANES
    index = np.arange(LANES)
    angle = 2.0 * np.pi * (np.outer(index, index) % LANES) / LANES
    cs, sn = np.cos(angle) / math.sqrt(whole), np.sin(angle) / math.sqrt(whole)
    weights = np.block([[cs, sn], [-sn, cs]]).astype(np.float32)
    high = weights.astype(ml_dtypes.bfloat16)
    low = (weights - high.astype(np.float32)).astype(ml_dtypes.bfloat16)
    angle = 2.0 * np.pi * np.outer(np.arange(rad), index) / whole
    twist = np.stack([np.cos(angle), np.sin(angle)]).astype(np.float32)
    per = rad // n
    quad = LANES // rad
    place = np.zeros((quad, taps * rad, taps * LANES), ml_dtypes.bfloat16)
    perm = np.zeros((n, 2 * LANES, 2 * quad * per), ml_dtypes.bfloat16)
    for j in range(n):
        for k in range(per):
            for s in range(quad):
                lane = quad * (j * per + k) + s
                for p in range(taps):
                    place[s, (j * taps + p) * per + k, p * LANES + lane] = 1
                for part in range(2):
                    perm[j, part * LANES + lane, (part * quad + s) * per + k] = 1
    return high, low, twist, place, perm


def shards(n, shards_t, observed, window_taps):
    frames = observed.shape[2]
    taps = window_taps.shape[0]
    rad = observed.shape[3] * n // LANES
    halo = 2 * (taps - 1)
    assert frames == 8 and halo <= frames <= 2 * halo and taps * rad == LANES
    constants = tables(n, rad, taps)
    hbm = pl.BlockSpec(memory_space=pltpu.HBM)
    vmem = pl.BlockSpec(memory_space=pltpu.VMEM)
    dma = pltpu.SemaphoreType.DMA
    results = pl.pallas_call(
        functools.partial(kernel, n, shards_t),
        out_shape=(jax.ShapeDtypeStruct(observed.shape, F32),) * 2,
        in_specs=[hbm] * 7,
        out_specs=(vmem, vmem),
        scratch_shapes=[
            pltpu.VMEM(observed.shape, F32),
            pltpu.VMEM(window_taps.shape, F32),
            *(pltpu.VMEM(constants[i].shape, constants[i].dtype) for i in (0, 1, 2, 3, 4)),
            dma((7,)),
            pltpu.VMEM((frames * 2 * rad, LANES), F32),
            pltpu.VMEM((2 * halo * 2 * rad, LANES), F32),
            pltpu.VMEM((taps * rad, LANES), F32),
            pltpu.VMEM((taps * rad, LANES), F32),
            pltpu.VMEM((frames * rad, LANES), F32),
            pltpu.VMEM((frames * rad, LANES), F32),
            pltpu.VMEM((2, frames * rad, LANES), F32),
            pltpu.VMEM((2, 2 * halo * rad, LANES), F32),
            pltpu.VMEM((4, 2, frames * rad, LANES), F32),
            pltpu.VMEM((2, 2, frames * rad, LANES), F32),
            pltpu.VMEM((2, 2 * frames * rad // n, LANES), F32),
            pltpu.VMEM((shards_t * STATS, LANES), F32),
            dma((n, frames // 2)),
            dma((n, frames // 2)),
            dma((n,)),
            dma((n,)),
            dma((2, n, frames // 2)),
            dma((2, n, frames // 2)),
            dma((shards_t,)),
            dma((shards_t,)),
        ],
        compiler_params=pltpu.CompilerParams(
            collective_id=0, has_side_effects=True, vmem_limit_bytes=56 * 1024 * 1024
        ),
        cost_estimate=pl.CostEstimate(flops=10**9, bytes_accessed=10**6, transcendentals=0),
    )(observed, window_taps, *(jnp.asarray(x) for x in constants))
    return pl.pallas_call(
        place_results,
        out_shape=(jax.ShapeDtypeStruct(observed.shape, F32),) * 2,
        in_specs=[hbm] * 2,
        out_specs=(hbm, hbm),
        scratch_shapes=[
            pltpu.VMEM(observed.shape[1:], F32),
            pltpu.VMEM(observed.shape[1:], F32),
            dma((2, 4)),
        ],
        compiler_params=pltpu.CompilerParams(vmem_limit_bytes=56 * 1024 * 1024),
    )(*results)


def solution(mesh):
    n, shards_t = mesh.shape["chan"], mesh.shape["tm"]
    block = P("pol", None, ("beam", "tm"), "chan")
    return jax.shard_map(
        functools.partial(shards, n, shards_t),
        mesh=mesh,
        in_specs=(block, P(None, "chan")),
        out_specs=(block, block),
        check_vma=False,
    )
```

```python
import functools
import math

import jax
import jax.numpy as jnp
import ml_dtypes
import numpy as np
from jax import lax
from jax.experimental import pallas as pl
from jax.experimental.pallas import tpu as pltpu
from jax.sharding import PartitionSpec as P

LANES = 128
MESH = pl.DeviceIdType.MESH
F32 = jnp.float32
BF16 = jnp.bfloat16
STATS = 16


def dft_rows(values):
    count = len(values)
    if count == 1:
        return values
    even = dft_rows(values[::2])
    odd = dft_rows(values[1::2])
    low, high = [], []
    for k in range(count // 2):
        er, ei = even[k]
        xr, xi = odd[k]
        if k == 0:
            tr, ti = xr, xi
        elif 4 * k == count:
            tr, ti = -xi, xr
        elif 8 * k == count:
            h = math.sqrt(0.5)
            tr, ti = h * (xr - xi), h * (xr + xi)
        elif 8 * k == 3 * count:
            h = math.sqrt(0.5)
            tr, ti = -h * (xr + xi), h * (xr - xi)
        else:
            cs = math.cos(2 * math.pi * k / count)
            sn = math.sin(2 * math.pi * k / count)
            tr, ti = cs * xr - sn * xi, sn * xr + cs * xi
        low.append((er + tr, ei + ti))
        high.append((er - tr, ei - ti))
    return low + high


def halves(value):
    high = value.astype(BF16)
    return high, (value - high.astype(F32)).astype(BF16)


def dot(left, right):
    return jnp.dot(left, right, preferred_element_type=F32)


def kernel(
    n,
    shards_t,
    obs_hbm,
    taps_hbm,
    whi_hbm,
    wlo_hbm,
    tw_hbm,
    place_hbm,
    perm_hbm,
    est_ref,
    res_ref,
    obs_ref,
    taps_ref,
    whi_ref,
    wlo_ref,
    tw_ref,
    place_ref,
    perm_ref,
    lo,
    xb,
    hb,
    tb,
    tp,
    zr,
    zi,
    yo,
    yh,
    dd,
    fr,
    es,
    ar,
    sx,
    rx,
    st,
    rt,
    sz,
    rz,
    sa,
    ra,
):
    loads = [
        pltpu.make_async_copy(src, dst, lo.at[i])
        for i, (src, dst) in enumerate(
            [
                (obs_hbm, obs_ref),
                (taps_hbm, taps_ref),
                (tw_hbm.at[:, : tw_ref.shape[1]], tw_ref),
                (whi_hbm, whi_ref),
                (wlo_hbm, wlo_ref),
                (place_hbm, place_ref),
                (perm_hbm, perm_ref),
            ]
        )
    ]
    for load in loads:
        load.start()
    frames = obs_ref.shape[2]
    taps = taps_ref.shape[0]
    lead = taps - 1
    halo = 2 * lead
    rad = zr.shape[0] // frames
    per = rad // n
    rows = 2 * per
    step = frames - halo
    pieces = [*range(step, frames - step, step), 0, frames - step]
    xs, hs, ts = frames * rows, 2 * halo * rows, taps * per
    c = lax.axis_index("chan")
    t = lax.axis_index("tm")
    has_prev = t > 0
    has_next = t < shards_t - 1

    barrier = pltpu.get_barrier_semaphore()
    for d in range(1, n):
        pl.semaphore_signal(
            barrier, inc=1, device_id={"chan": lax.rem(c + d, n)}, device_id_type=MESH
        )
    for d in range(1, shards_t):
        pl.semaphore_signal(
            barrier, inc=1, device_id={"tm": lax.rem(t + d, shards_t)}, device_id_type=MESH
        )

    loads[0].wait()
    for part in range(2):
        for k in range(per):
            xb[pl.ds(c * xs + part * per + k, frames, stride=rows), :] = obs_ref[
                0, part, :, k * LANES : (k + 1) * LANES
            ]
    loads[1].wait()
    for k in range(per):
        tb[pl.ds(c * ts + k, taps, stride=per), :] = taps_ref[:, k * LANES : (k + 1) * LANES]

    @pl.when(jnp.logical_not(has_prev))
    def _():
        for j in range(n):
            hb[j * hs : j * hs + halo * rows, :] = jnp.zeros((halo * rows, LANES), F32)

    @pl.when(jnp.logical_not(has_next))
    def _():
        for j in range(n):
            hb[j * hs + halo * rows : (j + 1) * hs, :] = jnp.zeros((halo * rows, LANES), F32)

    pl.semaphore_wait(barrier, n - 1 + shards_t - 1)

    def along_x(d, q):
        block = xb.at[pl.ds(pl.multiple_of(c * xs + pieces[q] * rows, 8), step * rows), :]
        return pltpu.make_async_remote_copy(
            src_ref=block,
            dst_ref=block,
            send_sem=sx.at[d, q],
            recv_sem=rx.at[d, q],
            device_id={"chan": lax.rem(c + d, n)},
            device_id_type=MESH,
        )

    def taps_x(d):
        block = tb.at[pl.ds(pl.multiple_of(c * ts, 8), ts), :]
        return pltpu.make_async_remote_copy(
            src_ref=block,
            dst_ref=block,
            send_sem=st.at[d],
            recv_sem=rt.at[d],
            device_id={"chan": lax.rem(c + d, n)},
            device_id_type=MESH,
        )

    def along_z(way, d, q, first, last):
        j = lax.rem(c - d + n, n)
        slot = first - (frames - halo) if way == 0 else halo + first
        size = (last - first) * rows
        return pltpu.make_async_remote_copy(
            src_ref=xb.at[pl.ds(pl.multiple_of(j * xs + first * rows, 8), size), :],
            dst_ref=hb.at[pl.ds(pl.multiple_of(j * hs + slot * rows, 8), size), :],
            send_sem=sz.at[way, d, q],
            recv_sem=rz.at[way, d, q],
            device_id={"tm": lax.rem(t + (1 if way == 0 else shards_t - 1), shards_t)},
            device_id_type=MESH,
        )

    spans = ((frames - halo, frames), (0, halo))
    forward = [[], []]
    for way in range(2):
        forward[way].append((0, 0) + spans[way])
        for d in range(1, n):
            for q, f in enumerate(pieces):
                if spans[way][0] <= f < spans[way][1]:
                    forward[way].append((d, q, f, f + step))
    sends_to = (has_next, has_prev)
    gets_from = (has_prev, has_next)

    def start_halo(d, q):
        for way in range(2):
            for move in forward[way]:
                if move[:2] == (d, q):

                    @pl.when(sends_to[way])
                    def _(way=way, move=move):
                        along_z(way, *move).start()

    for q in range(len(pieces)):
        for d in range(1, n):
            along_x(d, q).start()
    start_halo(0, 0)
    for d in range(1, n):
        taps_x(d).start()
    for load in loads[2:]:
        load.wait()
    for q in range(len(pieces)):
        for d in range(1, n):
            along_x(d, q).wait_recv()
            start_halo(d, q)
    def lanes_dft(real, imag):
        hi, lo = halves(jnp.concatenate([real, imag], axis=1))
        whi = whi_ref[...]
        return dot(hi, whi) + dot(lo, whi) + dot(hi, wlo_ref[...])

    def samples(src, stride, first):
        values = []
        for k in range(rad):
            base = (k // per) * stride + first * rows + k % per
            values.append(
                tuple(
                    src[pl.ds(base + part * per, frames, stride=rows), :] for part in range(2)
                )
            )
        for m, (re, im) in enumerate(dft_rows(values)):
            cs, sn = tw_ref[0, m : m + 1, :], tw_ref[1, m : m + 1, :]
            zr[pl.ds(m, frames, stride=rad), :] = re * cs - im * sn
            zi[pl.ds(m, frames, stride=rad), :] = re * sn + im * cs
        return lanes_dft(zr[...], zi[...])

    out = samples(xb, xs, 0)
    yo[0] = out[:, :LANES]
    yo[1] = out[:, LANES:]

    for d in range(1, n):
        taps_x(d).wait_recv()
    turned = tb[...].T
    first = turned.astype(BF16)
    rest = turned - first.astype(F32)
    second = rest.astype(BF16)
    third = (rest - second.astype(F32)).astype(BF16)
    placed = jnp.zeros((rad, taps * LANES), F32)
    for s in range(LANES // rad):
        rng = slice(s * rad, (s + 1) * rad)
        for piece in (third, second, first):
            placed = placed + dot(piece[rng, :], place_ref[s])
    for p in range(taps):
        tp[p * rad : (p + 1) * rad, :] = placed[:, p * LANES : (p + 1) * LANES]

    for way in range(2):

        @pl.when(gets_from[way])
        def _(way=way):
            for move in forward[way]:
                along_z(way, *move).wait_recv()

    shift = 2 * halo - frames

    def halo_step(i, carry):
        begin = i * shift
        out = samples(hb, hs, begin)
        at = pl.ds(pl.multiple_of(begin * rad, 8), frames * rad)
        yh[0, at, :] = out[:, :LANES]
        yh[1, at, :] = out[:, LANES:]
        return carry

    lax.fori_loop(0, 2, halo_step, 0)

    keep_prev = jnp.where(has_prev, 1.0, 0.0).astype(F32)
    keep_next = jnp.where(has_next, 1.0, 0.0).astype(F32)
    chunks = rad // 8

    def window_step(i, carry):
        s0, s1 = carry
        part = i // chunks
        ch = i % chunks

        def at(f):
            return pl.ds(pl.multiple_of(f * rad + ch * 8, 8), 8)

        def signal(f):
            if f < 0:
                return yh[part, at(f + halo), :]
            if f < frames:
                return yo[part, at(f), :]
            return yh[part, at(f - frames + halo), :]

        w = [tp[at(p), :] for p in range(taps)]

        def ahead(x, f):
            return sum(w[p] * x[f + p] for p in range(1, taps)) + w[0] * x[f]

        def behind(x, f):
            return sum(w[p] * x[f - p] for p in range(1, taps)) + w[0] * x[f]

        y = {f: signal(f) for f in range(-halo, frames + halo)}
        g = {f: ahead(y, f) for f in range(-halo, frames + lead)}
        g = {f: (v * keep_prev if f < 0 else v) for f, v in g.items()}
        v = {f: behind(g, f) for f in range(-lead, frames + lead)}
        v = {f: (x * keep_next if f >= frames else x) for f, x in v.items()}
        z = {f: ahead(v, f) for f in range(-lead, frames)}
        z = {f: (x * keep_prev if f < 0 else x) for f, x in z.items()}
        for f in range(frames):
            dd[0, part, at(f), :] = g[f]
            dd[1, part, at(f), :] = z[f]
            dd[2, part, at(f), :] = v[f]
            dd[3, part, at(f), :] = behind(z, f)
            s0 = s0 + g[f] * g[f]
            s1 = s1 + v[f] * v[f]
        return s0, s1

    zero = jnp.zeros((8, LANES), F32)
    s0, s1 = lax.fori_loop(0, 2 * chunks, window_step, (zero, zero))
    s0 = jnp.sum(s0, keepdims=True)
    s1 = jnp.sum(s1, keepdims=True)
    center = jnp.where(s1 > 0, s0 / jnp.where(s1 > 0, s1, 1.0), 0.0)

    def moment_step(i, carry):
        pp, pz, zz, qq, qu, uu = carry
        part = i // chunks
        ch = i % chunks
        for f in range(frames):
            at = pl.ds(pl.multiple_of(f * rad + ch * 8, 8), 8)
            z, u = dd[1, part, at, :], dd[3, part, at, :]
            p = dd[0, part, at, :] - center * z
            q = dd[2, part, at, :] - center * u
            pp, pz, zz = pp + p * p, pz + p * z, zz + z * z
            qq, qu, uu = qq + q * q, qu + q * u, uu + u * u
        return pp, pz, zz, qq, qu, uu

    moments = lax.fori_loop(0, 2 * chunks, moment_step, (zero,) * 6)
    moments = [jnp.sum(x, keepdims=True) for x in moments]
    line = jnp.concatenate(
        [jnp.broadcast_to(x, (1, LANES)) for x in [s0, s1, center] + moments]
        + [jnp.zeros((STATS - 9, LANES), F32)],
        axis=0,
    )
    mine = pl.ds(pl.multiple_of(t * STATS, 8), STATS)
    ar[mine, :] = line

    def sums_to(d):
        return pltpu.make_async_remote_copy(
            src_ref=ar.at[mine, :],
            dst_ref=ar.at[mine, :],
            send_sem=sa.at[d],
            recv_sem=ra.at[d],
            device_id={"tm": lax.rem(t + d, shards_t)},
            device_id_type=MESH,
        )

    for d in range(1, shards_t):
        sums_to(d).start()

    def spectrum_step(a, carry):
        out = lanes_dft(dd[2 + a, 0], -dd[2 + a, 1])
        for f in range(frames):
            at = slice(f * rad, (f + 1) * rad)
            re, im = out[at, :LANES], out[at, LANES:]
            zr[at, :] = re * tw_ref[0] - im * tw_ref[1]
            zi[at, :] = re * tw_ref[1] + im * tw_ref[0]
        values = [
            (zr[pl.ds(m, frames, stride=rad), :], zi[pl.ds(m, frames, stride=rad), :])
            for m in range(rad)
        ]
        for k, (re, im) in enumerate(dft_rows(values)):
            fr[a, 0, k * frames : (k + 1) * frames, :] = re
            fr[a, 1, k * frames : (k + 1) * frames, :] = im
        hi, lo = halves(jnp.concatenate([dd[a, 0], dd[a, 1]], axis=1))
        perm = perm_ref[c]
        moved = dot(hi, perm) + dot(lo, perm)
        quad = LANES // rad
        for h in range(frames // quad):
            flat = moved[h * LANES : (h + 1) * LANES, :].T
            for part in range(2):
                for f in range(quad):
                    joined = jnp.concatenate(
                        [
                            flat[
                                (part * quad + s) * per : (part * quad + s + 1) * per,
                                f * rad : (f + 1) * rad,
                            ]
                            for s in range(quad)
                        ],
                        axis=1,
                    )
                    row = (part * frames + h * quad + f) * per
                    es[a, row : row + per, :] = joined
        return carry

    lax.fori_loop(0, 2, spectrum_step, 0)

    for d in range(1, shards_t):
        sums_to(d).wait_recv()

    def total(i):
        return sum(ar[s * STATS + i : s * STATS + i + 1, :] for s in range(shards_t))

    gamma0 = total(0)
    step0 = gamma0 / total(1)
    gamma1 = jnp.zeros((1, LANES), F32)
    grown = jnp.zeros((1, LANES), F32)
    for s in range(shards_t):
        line = ar[s * STATS : (s + 1) * STATS, :]
        away = step0 - line[2:3]
        gamma1 = gamma1 + (line[3:4] - away * (2.0 * line[4:5] - away * line[5:6]))
        grown = grown + (line[6:7] - away * (2.0 * line[7:8] - away * line[8:9]))
    ratio = gamma1 / gamma0
    step1 = gamma1 / (grown - ratio * gamma1 / step0)
    near = step0 + step1 * (1.0 + ratio)
    far = step0 * step1

    for part in range(2):
        for k in range(per):
            at = pl.ds(pl.multiple_of((c * per + k) * frames, 8), frames)
            change = near * fr[0, part, at, :] - far * fr[1, part, at, :]
            here = obs_ref[0, part, :, k * LANES : (k + 1) * LANES]
            res_ref[0, part, :, k * LANES : (k + 1) * LANES] = (
                here - change if part == 0 else here + change
            )
            at = pl.ds(part * frames * per + k, frames, stride=per)
            est_ref[0, part, :, k * LANES : (k + 1) * LANES] = near * es.at[0][at, :] - far * es.at[
                1
            ][at, :]

    for d in range(1, n):
        for q in range(len(pieces)):
            along_x(d, q).wait_send()
        taps_x(d).wait_send()
    for d in range(1, shards_t):
        sums_to(d).wait_send()
    for way in range(2):

        @pl.when(sends_to[way])
        def _(way=way):
            for move in forward[way]:
                along_z(way, *move).wait_send()


def place_results(est_in, res_in, est_out, res_out, sems):
    moves = [
        pltpu.make_async_copy(src.at[:, part], dst.at[:, part], sems.at[2 * i + part])
        for i, (src, dst) in enumerate([(est_in, est_out), (res_in, res_out)])
        for part in range(2)
    ]
    for move in moves:
        move.start()
    for move in moves:
        move.wait()


def tables(n, rad, taps):
    whole = rad * LANES
    index = np.arange(LANES)
    angle = 2.0 * np.pi * (np.outer(index, index) % LANES) / LANES
    cs, sn = np.cos(angle) / math.sqrt(whole), np.sin(angle) / math.sqrt(whole)
    weights = np.block([[cs, sn], [-sn, cs]]).astype(np.float32)
    high = weights.astype(ml_dtypes.bfloat16)
    low = (weights - high.astype(np.float32)).astype(ml_dtypes.bfloat16)
    angle = 2.0 * np.pi * np.outer(np.arange(rad), index) / whole
    twist = np.stack([np.cos(angle), np.sin(angle)]).astype(np.float32)
    per = rad // n
    quad = LANES // rad
    place = np.zeros((quad, taps * rad, taps * LANES), ml_dtypes.bfloat16)
    perm = np.zeros((n, 2 * LANES, 2 * quad * per), ml_dtypes.bfloat16)
    for j in range(n):
        for k in range(per):
            for s in range(quad):
                lane = quad * (j * per + k) + s
                for p in range(taps):
                    place[s, (j * taps + p) * per + k, p * LANES + lane] = 1
                for part in range(2):
                    perm[j, part * LANES + lane, (part * quad + s) * per + k] = 1
    return high, low, twist, place, perm


def shards(n, shards_t, observed, window_taps):
    frames = observed.shape[2]
    taps = window_taps.shape[0]
    rad = observed.shape[3] * n // LANES
    halo = 2 * (taps - 1)
    assert frames == 8 and halo <= frames <= 2 * halo and taps * rad == LANES
    constants = tables(n, rad, taps)
    shapes = [x.shape for x in constants]
    constants = list(constants)
    constants[2] = np.pad(constants[2], ((0, 0), (0, 1024), (0, 0)))
    hbm = pl.BlockSpec(memory_space=pltpu.HBM)
    vmem = pl.BlockSpec(memory_space=pltpu.VMEM)
    dma = pltpu.SemaphoreType.DMA
    results = pl.pallas_call(
        functools.partial(kernel, n, shards_t),
        out_shape=(jax.ShapeDtypeStruct(observed.shape, F32),) * 2,
        in_specs=[hbm] * 7,
        out_specs=(vmem, vmem),
        scratch_shapes=[
            pltpu.VMEM(observed.shape, F32),
            pltpu.VMEM(window_taps.shape, F32),
            *(pltpu.VMEM(shapes[i], constants[i].dtype) for i in (0, 1, 2, 3, 4)),
            dma((7,)),
            pltpu.VMEM((frames * 2 * rad, LANES), F32),
            pltpu.VMEM((2 * halo * 2 * rad, LANES), F32),
            pltpu.VMEM((taps * rad, LANES), F32),
            pltpu.VMEM((taps * rad, LANES), F32),
            pltpu.VMEM((frames * rad, LANES), F32),
            pltpu.VMEM((frames * rad, LANES), F32),
            pltpu.VMEM((2, frames * rad, LANES), F32),
            pltpu.VMEM((2, 2 * halo * rad, LANES), F32),
            pltpu.VMEM((4, 2, frames * rad, LANES), F32),
            pltpu.VMEM((2, 2, frames * rad, LANES), F32),
            pltpu.VMEM((2, 2 * frames * rad // n, LANES), F32),
            pltpu.VMEM((shards_t * STATS, LANES), F32),
            dma((n, frames // 2)),
            dma((n, frames // 2)),
            dma((n,)),
            dma((n,)),
            dma((2, n, frames // 2)),
            dma((2, n, frames // 2)),
            dma((shards_t,)),
            dma((shards_t,)),
        ],
        compiler_params=pltpu.CompilerParams(
            collective_id=0, has_side_effects=True, vmem_limit_bytes=56229888
        ),
        cost_estimate=pl.CostEstimate(flops=10**9, bytes_accessed=10**6, transcendentals=0),
    )(observed, window_taps, *(jnp.asarray(x) for x in constants))
    return pl.pallas_call(
        place_results,
        out_shape=(jax.ShapeDtypeStruct(observed.shape, F32),) * 2,
        in_specs=[vmem] * 2,
        out_specs=(hbm, hbm),
        scratch_shapes=[
            dma((4,)),
        ],
        compiler_params=pltpu.CompilerParams(vmem_limit_bytes=4 * 1024 * 1024),
    )(*results)


def solution(mesh):
    n, shards_t = mesh.shape["chan"], mesh.shape["tm"]
    block = P("pol", None, ("beam", "tm"), "chan")
    return jax.shard_map(
        functools.partial(shards, n, shards_t),
        mesh=mesh,
        in_specs=(block, P(None, "chan")),
        out_specs=(block, block),
        check_vma=False,
    )
```

```python
import functools
import math

import jax
import jax.numpy as jnp
import ml_dtypes
import numpy as np
from jax import lax
from jax.experimental import pallas as pl
from jax.experimental.pallas import tpu as pltpu
from jax.sharding import PartitionSpec as P

LANES = 128
MESH = pl.DeviceIdType.MESH
F32 = jnp.float32
BF16 = jnp.bfloat16
STATS = 16


def dft_rows(values):
    count = len(values)
    if count == 1:
        return values
    even = dft_rows(values[::2])
    odd = dft_rows(values[1::2])
    low, high = [], []
    for k in range(count // 2):
        er, ei = even[k]
        xr, xi = odd[k]
        if k == 0:
            tr, ti = xr, xi
        elif 4 * k == count:
            tr, ti = -xi, xr
        elif 8 * k == count:
            h = math.sqrt(0.5)
            tr, ti = h * (xr - xi), h * (xr + xi)
        elif 8 * k == 3 * count:
            h = math.sqrt(0.5)
            tr, ti = -h * (xr + xi), h * (xr - xi)
        else:
            cs = math.cos(2 * math.pi * k / count)
            sn = math.sin(2 * math.pi * k / count)
            tr, ti = cs * xr - sn * xi, sn * xr + cs * xi
        low.append((er + tr, ei + ti))
        high.append((er - tr, ei - ti))
    return low + high


def halves(value):
    high = value.astype(BF16)
    return high, (value - high.astype(F32)).astype(BF16)


def dot(left, right):
    return jnp.dot(left, right, preferred_element_type=F32)


def kernel(
    n,
    shards_t,
    obs_hbm,
    taps_hbm,
    whi_hbm,
    wlo_hbm,
    tw_hbm,
    place_hbm,
    perm_hbm,
    est_ref,
    res_ref,
    obs_ref,
    taps_ref,
    whi_ref,
    wlo_ref,
    tw_ref,
    place_ref,
    perm_ref,
    lo,
    xb,
    hb,
    tb,
    tp,
    zr,
    zi,
    yo,
    yh,
    dd,
    fr,
    es,
    ar,
    sx,
    rx,
    st,
    rt,
    sz,
    rz,
    sa,
    ra,
):
    loads = [
        pltpu.make_async_copy(src, dst, lo.at[i])
        for i, (src, dst) in enumerate(
            [
                (obs_hbm, obs_ref),
                (taps_hbm, taps_ref),
                (tw_hbm.at[:, : tw_ref.shape[1]], tw_ref),
                (whi_hbm, whi_ref),
                (wlo_hbm, wlo_ref),
                (place_hbm, place_ref),
                (perm_hbm, perm_ref),
            ]
        )
    ]
    for load in loads:
        load.start()
    frames = obs_ref.shape[2]
    taps = taps_ref.shape[0]
    lead = taps - 1
    halo = 2 * lead
    rad = zr.shape[0] // frames
    per = rad // n
    rows = 2 * per
    step = frames - halo
    pieces = [*range(step, frames - step, step), 0, frames - step]
    xs, hs, ts = frames * rows, 2 * halo * rows, taps * per
    c = lax.axis_index("chan")
    t = lax.axis_index("tm")
    has_prev = t > 0
    has_next = t < shards_t - 1

    barrier = pltpu.get_barrier_semaphore()
    for d in range(1, n):
        pl.semaphore_signal(
            barrier, inc=1, device_id={"chan": lax.rem(c + d, n)}, device_id_type=MESH
        )
    for d in range(1, shards_t):
        pl.semaphore_signal(
            barrier, inc=1, device_id={"tm": lax.rem(t + d, shards_t)}, device_id_type=MESH
        )

    loads[0].wait()
    for part in range(2):
        for k in range(per):
            xb[pl.ds(c * xs + part * per + k, frames, stride=rows), :] = obs_ref[
                0, part, :, k * LANES : (k + 1) * LANES
            ]
    loads[1].wait()
    for k in range(per):
        tb[pl.ds(c * ts + k, taps, stride=per), :] = taps_ref[:, k * LANES : (k + 1) * LANES]

    @pl.when(jnp.logical_not(has_prev))
    def _():
        for j in range(n):
            hb[j * hs : j * hs + halo * rows, :] = jnp.zeros((halo * rows, LANES), F32)

    @pl.when(jnp.logical_not(has_next))
    def _():
        for j in range(n):
            hb[j * hs + halo * rows : (j + 1) * hs, :] = jnp.zeros((halo * rows, LANES), F32)

    pl.semaphore_wait(barrier, n - 1 + shards_t - 1)

    def along_x(d, q):
        block = xb.at[pl.ds(pl.multiple_of(c * xs + pieces[q] * rows, 8), step * rows), :]
        return pltpu.make_async_remote_copy(
            src_ref=block,
            dst_ref=block,
            send_sem=sx.at[d, q],
            recv_sem=rx.at[d, q],
            device_id={"chan": lax.rem(c + d, n)},
            device_id_type=MESH,
        )

    def taps_x(d):
        block = tb.at[pl.ds(pl.multiple_of(c * ts, 8), ts), :]
        return pltpu.make_async_remote_copy(
            src_ref=block,
            dst_ref=block,
            send_sem=st.at[d],
            recv_sem=rt.at[d],
            device_id={"chan": lax.rem(c + d, n)},
            device_id_type=MESH,
        )

    def along_z(way, d, q, first, last):
        j = lax.rem(c - d + n, n)
        slot = first - (frames - halo) if way == 0 else halo + first
        size = (last - first) * rows
        return pltpu.make_async_remote_copy(
            src_ref=xb.at[pl.ds(pl.multiple_of(j * xs + first * rows, 8), size), :],
            dst_ref=hb.at[pl.ds(pl.multiple_of(j * hs + slot * rows, 8), size), :],
            send_sem=sz.at[way, d, q],
            recv_sem=rz.at[way, d, q],
            device_id={"tm": lax.rem(t + (1 if way == 0 else shards_t - 1), shards_t)},
            device_id_type=MESH,
        )

    spans = ((frames - halo, frames), (0, halo))
    forward = [[], []]
    for way in range(2):
        forward[way].append((0, 0) + spans[way])
        for d in range(1, n):
            for q, f in enumerate(pieces):
                if spans[way][0] <= f < spans[way][1]:
                    forward[way].append((d, q, f, f + step))
    sends_to = (has_next, has_prev)
    gets_from = (has_prev, has_next)

    def start_halo(d, q):
        for way in range(2):
            for move in forward[way]:
                if move[:2] == (d, q):

                    @pl.when(sends_to[way])
                    def _(way=way, move=move):
                        along_z(way, *move).start()

    for q in range(len(pieces)):
        for d in range(1, n):
            along_x(d, q).start()
    start_halo(0, 0)
    for d in range(1, n):
        taps_x(d).start()
    for load in loads[2:]:
        load.wait()
    for q in range(len(pieces)):
        for d in range(1, n):
            along_x(d, q).wait_recv()
            start_halo(d, q)
    def lanes_dft(real, imag):
        hi, lo = halves(jnp.concatenate([real, imag], axis=1))
        whi = whi_ref[...]
        return dot(hi, whi) + dot(lo, whi) + dot(hi, wlo_ref[...])

    def samples(src, stride, first):
        values = []
        for k in range(rad):
            base = (k // per) * stride + first * rows + k % per
            values.append(
                tuple(
                    src[pl.ds(base + part * per, frames, stride=rows), :] for part in range(2)
                )
            )
        for m, (re, im) in enumerate(dft_rows(values)):
            cs, sn = tw_ref[0, m : m + 1, :], tw_ref[1, m : m + 1, :]
            zr[pl.ds(m, frames, stride=rad), :] = re * cs - im * sn
            zi[pl.ds(m, frames, stride=rad), :] = re * sn + im * cs
        return lanes_dft(zr[...], zi[...])

    out = samples(xb, xs, 0)
    yo[0] = out[:, :LANES]
    yo[1] = out[:, LANES:]

    for d in range(1, n):
        taps_x(d).wait_recv()
    turned = tb[...].T
    first = turned.astype(BF16)
    rest = turned - first.astype(F32)
    second = rest.astype(BF16)
    third = (rest - second.astype(F32)).astype(BF16)
    placed = jnp.zeros((rad, taps * LANES), F32)
    for s in range(LANES // rad):
        rng = slice(s * rad, (s + 1) * rad)
        for piece in (third, second, first):
            placed = placed + dot(piece[rng, :], place_ref[s])
    for p in range(taps):
        tp[p * rad : (p + 1) * rad, :] = placed[:, p * LANES : (p + 1) * LANES]

    for way in range(2):

        @pl.when(gets_from[way])
        def _(way=way):
            for move in forward[way]:
                along_z(way, *move).wait_recv()

    shift = 2 * halo - frames

    def halo_step(i, carry):
        begin = i * shift
        out = samples(hb, hs, begin)
        at = pl.ds(pl.multiple_of(begin * rad, 8), frames * rad)
        yh[0, at, :] = out[:, :LANES]
        yh[1, at, :] = out[:, LANES:]
        return carry

    lax.fori_loop(0, 2, halo_step, 0)

    keep_prev = jnp.where(has_prev, 1.0, 0.0).astype(F32)
    keep_next = jnp.where(has_next, 1.0, 0.0).astype(F32)
    chunks = rad // 8

    def window_step(i, carry):
        s0, s1 = carry
        part = i // chunks
        ch = i % chunks

        def at(f):
            return pl.ds(pl.multiple_of(f * rad + ch * 8, 8), 8)

        def signal(f):
            if f < 0:
                return yh[part, at(f + halo), :]
            if f < frames:
                return yo[part, at(f), :]
            return yh[part, at(f - frames + halo), :]

        w = [tp[at(p), :] for p in range(taps)]

        def ahead(x, f):
            return sum(w[p] * x[f + p] for p in range(1, taps)) + w[0] * x[f]

        def behind(x, f):
            return sum(w[p] * x[f - p] for p in range(1, taps)) + w[0] * x[f]

        y = {f: signal(f) for f in range(-halo, frames + halo)}
        g = {f: ahead(y, f) for f in range(-halo, frames + lead)}
        g = {f: (v * keep_prev if f < 0 else v) for f, v in g.items()}
        v = {f: behind(g, f) for f in range(-lead, frames + lead)}
        v = {f: (x * keep_next if f >= frames else x) for f, x in v.items()}
        z = {f: ahead(v, f) for f in range(-lead, frames)}
        z = {f: (x * keep_prev if f < 0 else x) for f, x in z.items()}
        for f in range(frames):
            dd[0, part, at(f), :] = g[f]
            dd[1, part, at(f), :] = z[f]
            dd[2, part, at(f), :] = v[f]
            dd[3, part, at(f), :] = behind(z, f)
            s0 = s0 + g[f] * g[f]
            s1 = s1 + v[f] * v[f]
        return s0, s1

    zero = jnp.zeros((8, LANES), F32)
    s0, s1 = lax.fori_loop(0, 2 * chunks, window_step, (zero, zero))
    s0 = jnp.sum(s0, keepdims=True)
    s1 = jnp.sum(s1, keepdims=True)
    center = jnp.where(s1 > 0, s0 / jnp.where(s1 > 0, s1, 1.0), 0.0)

    def moment_step(i, carry):
        pp, pz, zz, qq, qu, uu = carry
        part = i // chunks
        ch = i % chunks
        for f in range(frames):
            at = pl.ds(pl.multiple_of(f * rad + ch * 8, 8), 8)
            z, u = dd[1, part, at, :], dd[3, part, at, :]
            p = dd[0, part, at, :] - center * z
            q = dd[2, part, at, :] - center * u
            pp, pz, zz = pp + p * p, pz + p * z, zz + z * z
            qq, qu, uu = qq + q * q, qu + q * u, uu + u * u
        return pp, pz, zz, qq, qu, uu

    moments = lax.fori_loop(0, 2 * chunks, moment_step, (zero,) * 6)
    moments = [jnp.sum(x, keepdims=True) for x in moments]
    line = jnp.concatenate(
        [jnp.broadcast_to(x, (1, LANES)) for x in [s0, s1, center] + moments]
        + [jnp.zeros((STATS - 9, LANES), F32)],
        axis=0,
    )
    mine = pl.ds(pl.multiple_of(t * STATS, 8), STATS)
    ar[mine, :] = line

    def sums_to(d):
        return pltpu.make_async_remote_copy(
            src_ref=ar.at[mine, :],
            dst_ref=ar.at[mine, :],
            send_sem=sa.at[d],
            recv_sem=ra.at[d],
            device_id={"tm": lax.rem(t + d, shards_t)},
            device_id_type=MESH,
        )

    for d in range(1, shards_t):
        sums_to(d).start()

    def spectrum_step(a, carry):
        out = lanes_dft(dd[2 + a, 0], -dd[2 + a, 1])
        for f in range(frames):
            at = slice(f * rad, (f + 1) * rad)
            re, im = out[at, :LANES], out[at, LANES:]
            zr[at, :] = re * tw_ref[0] - im * tw_ref[1]
            zi[at, :] = re * tw_ref[1] + im * tw_ref[0]
        values = [
            (zr[pl.ds(m, frames, stride=rad), :], zi[pl.ds(m, frames, stride=rad), :])
            for m in range(rad)
        ]
        for k, (re, im) in enumerate(dft_rows(values)):
            fr[a, 0, k * frames : (k + 1) * frames, :] = re
            fr[a, 1, k * frames : (k + 1) * frames, :] = im
        hi, lo = halves(jnp.concatenate([dd[a, 0], dd[a, 1]], axis=1))
        perm = perm_ref[c]
        moved = dot(hi, perm) + dot(lo, perm)
        quad = LANES // rad
        for h in range(frames // quad):
            flat = moved[h * LANES : (h + 1) * LANES, :].T
            for part in range(2):
                for f in range(quad):
                    joined = jnp.concatenate(
                        [
                            flat[
                                (part * quad + s) * per : (part * quad + s + 1) * per,
                                f * rad : (f + 1) * rad,
                            ]
                            for s in range(quad)
                        ],
                        axis=1,
                    )
                    row = (part * frames + h * quad + f) * per
                    es[a, row : row + per, :] = joined
        return carry

    lax.fori_loop(0, 2, spectrum_step, 0)

    for d in range(1, shards_t):
        sums_to(d).wait_recv()

    def total(i):
        return sum(ar[s * STATS + i : s * STATS + i + 1, :] for s in range(shards_t))

    gamma0 = total(0)
    step0 = gamma0 / total(1)
    gamma1 = jnp.zeros((1, LANES), F32)
    grown = jnp.zeros((1, LANES), F32)
    for s in range(shards_t):
        line = ar[s * STATS : (s + 1) * STATS, :]
        away = step0 - line[2:3]
        gamma1 = gamma1 + (line[3:4] - away * (2.0 * line[4:5] - away * line[5:6]))
        grown = grown + (line[6:7] - away * (2.0 * line[7:8] - away * line[8:9]))
    ratio = gamma1 / gamma0
    step1 = gamma1 / (grown - ratio * gamma1 / step0)
    near = step0 + step1 * (1.0 + ratio)
    far = step0 * step1

    for part in range(2):
        for k in range(per):
            at = pl.ds(pl.multiple_of((c * per + k) * frames, 8), frames)
            change = near * fr[0, part, at, :] - far * fr[1, part, at, :]
            here = obs_ref[0, part, :, k * LANES : (k + 1) * LANES]
            res_ref[0, part, :, k * LANES : (k + 1) * LANES] = (
                here - change if part == 0 else here + change
            )
            at = pl.ds(part * frames * per + k, frames, stride=per)
            est_ref[0, part, :, k * LANES : (k + 1) * LANES] = near * es.at[0][at, :] - far * es.at[
                1
            ][at, :]

    for d in range(1, n):
        for q in range(len(pieces)):
            along_x(d, q).wait_send()
        taps_x(d).wait_send()
    for d in range(1, shards_t):
        sums_to(d).wait_send()
    for way in range(2):

        @pl.when(sends_to[way])
        def _(way=way):
            for move in forward[way]:
                along_z(way, *move).wait_send()


def place_results(est_in, res_in, est_out, res_out, sems):
    moves = [
        pltpu.make_async_copy(src.at[:, part], dst.at[:, part], sems.at[2 * i + part])
        for i, (src, dst) in enumerate([(est_in, est_out), (res_in, res_out)])
        for part in range(2)
    ]
    for move in moves:
        move.start()
    for move in moves:
        move.wait()


def tables(n, rad, taps):
    whole = rad * LANES
    index = np.arange(LANES)
    angle = 2.0 * np.pi * (np.outer(index, index) % LANES) / LANES
    cs, sn = np.cos(angle) / math.sqrt(whole), np.sin(angle) / math.sqrt(whole)
    weights = np.block([[cs, sn], [-sn, cs]]).astype(np.float32)
    high = weights.astype(ml_dtypes.bfloat16)
    low = (weights - high.astype(np.float32)).astype(ml_dtypes.bfloat16)
    angle = 2.0 * np.pi * np.outer(np.arange(rad), index) / whole
    twist = np.stack([np.cos(angle), np.sin(angle)]).astype(np.float32)
    per = rad // n
    quad = LANES // rad
    place = np.zeros((quad, taps * rad, taps * LANES), ml_dtypes.bfloat16)
    perm = np.zeros((n, 2 * LANES, 2 * quad * per), ml_dtypes.bfloat16)
    for j in range(n):
        for k in range(per):
            for s in range(quad):
                lane = quad * (j * per + k) + s
                for p in range(taps):
                    place[s, (j * taps + p) * per + k, p * LANES + lane] = 1
                for part in range(2):
                    perm[j, part * LANES + lane, (part * quad + s) * per + k] = 1
    return high, low, twist, place, perm


def shards(n, shards_t, observed, window_taps):
    frames = observed.shape[2]
    taps = window_taps.shape[0]
    rad = observed.shape[3] * n // LANES
    halo = 2 * (taps - 1)
    assert frames == 8 and halo <= frames <= 2 * halo and taps * rad == LANES
    constants = tables(n, rad, taps)
    shapes = [x.shape for x in constants]
    constants = list(constants)
    constants[2] = np.pad(constants[2], ((0, 0), (0, 1024), (0, 0)))
    hbm = pl.BlockSpec(memory_space=pltpu.HBM)
    vmem = pl.BlockSpec(memory_space=pltpu.VMEM)
    dma = pltpu.SemaphoreType.DMA
    results = pl.pallas_call(
        functools.partial(kernel, n, shards_t),
        out_shape=(jax.ShapeDtypeStruct(observed.shape, F32),) * 2,
        in_specs=[hbm] * 7,
        out_specs=(vmem, vmem),
        scratch_shapes=[
            pltpu.VMEM(observed.shape, F32),
            pltpu.VMEM(window_taps.shape, F32),
            *(pltpu.VMEM(shapes[i], constants[i].dtype) for i in (0, 1, 2, 3, 4)),
            dma((7,)),
            pltpu.VMEM((frames * 2 * rad, LANES), F32),
            pltpu.VMEM((2 * halo * 2 * rad, LANES), F32),
            pltpu.VMEM((taps * rad, LANES), F32),
            pltpu.VMEM((taps * rad, LANES), F32),
            pltpu.VMEM((frames * rad, LANES), F32),
            pltpu.VMEM((frames * rad, LANES), F32),
            pltpu.VMEM((2, frames * rad, LANES), F32),
            pltpu.VMEM((2, 2 * halo * rad, LANES), F32),
            pltpu.VMEM((4, 2, frames * rad, LANES), F32),
            pltpu.VMEM((2, 2, frames * rad, LANES), F32),
            pltpu.VMEM((2, 2 * frames * rad // n, LANES), F32),
            pltpu.VMEM((shards_t * STATS, LANES), F32),
            dma((n, frames // 2)),
            dma((n, frames // 2)),
            dma((n,)),
            dma((n,)),
            dma((2, n, frames // 2)),
            dma((2, n, frames // 2)),
            dma((shards_t,)),
            dma((shards_t,)),
        ],
        compiler_params=pltpu.CompilerParams(
            collective_id=0, has_side_effects=True, vmem_limit_bytes=56262656
        ),
        cost_estimate=pl.CostEstimate(flops=10**9, bytes_accessed=10**6, transcendentals=0),
    )(observed, window_taps, *(jnp.asarray(x) for x in constants))
    return pl.pallas_call(
        place_results,
        out_shape=(jax.ShapeDtypeStruct(observed.shape, F32),) * 2,
        in_specs=[vmem] * 2,
        out_specs=(hbm, hbm),
        scratch_shapes=[
            dma((4,)),
        ],
        compiler_params=pltpu.CompilerParams(vmem_limit_bytes=4 * 1024 * 1024),
    )(*results)


def solution(mesh):
    n, shards_t = mesh.shape["chan"], mesh.shape["tm"]
    block = P("pol", None, ("beam", "tm"), "chan")
    return jax.shard_map(
        functools.partial(shards, n, shards_t),
        mesh=mesh,
        in_specs=(block, P(None, "chan")),
        out_specs=(block, block),
        check_vma=False,
    )
```
